32 devices in a mesh: tm: 4 (over y, x), rows: 8 (over z, core).
Axes of the slice: x: 2, y: 2, z: 4, core: 2. Of those that a mesh axis runs over, the one named last changes fastest.
Arguments:
- features: bfloat16 [4, 8, 16, 96, 384], P(None, 'tm', 'rows'), may hold values from -6 to 6
- frame_counts: int32 [4], replicated, may hold values from 1 to 8, as said below
- owner_order: int32 [4], replicated, may hold values from 0 to 3, each once
- first_gain: float32 [384], replicated, may hold values from 0.1 to 1.9
- first_kernel: bfloat16 [3, 3, 3, 384, 384], replicated, may hold values from -0.0625 to 0.0625
- first_bias: float32 [384], replicated, may hold values from -3 to 3
- second_gain: float32 [384], replicated, may hold values from 0.1 to 1.9
- second_kernel: bfloat16 [3, 3, 3, 384, 384], replicated, may hold values from -0.0625 to 0.0625
- second_bias: float32 [384], replicated, may hold values from -3 to 3
Outputs:
- student_latents: bfloat16 [4, 8, 16, 96, 384], P('tm', None, None, 'rows')
The draws below stay inside these ranges and needn't reach their ends.
Inputs may be any that keep to these rules, and one draw needn't show every extreme that they name: `frame_counts`: at least one clip has exactly 8 frames. `owner_order`: each clip appears once.
All inputs are finite; a program needn't handle non-finite values.
Results may differ from the reference program's by a relative error of at most 0.008.
Values may be sent and summed in bfloat16 or wider, within the bound.
No kernel may reach another device: no remote copies, remote signals or barrier semaphores. Data moves between devices by JAX's collectives and lax.ppermute only.
A program may use at most 128 MiB of HBM per device.

```python
import jax
import jax.numpy as jnp
from jax import lax

C = 384
W = 96
CLIPS = 4
FRAMES = 8
H = 16


def draw_frame_counts(key, part):
    first_key, second_key = jax.random.split(jax.random.fold_in(key, 17))
    counted = jax.random.randint(first_key, (CLIPS,), 1, FRAMES + 1)
    longest = jax.random.randint(second_key, (), 0, CLIPS)
    return jnp.where(jnp.arange(CLIPS) == longest, FRAMES, counted).astype(jnp.int32)


def shard_levels(own_key, dims, cuts, smallest, largest):
    level, own = 1.0, jax.random.fold_in(own_key, 6)
    for axis_at, shards_of in cuts:
        draws = jnp.exp(jax.random.uniform(jax.random.fold_in(own, axis_at), (shards_of,), jnp.float32, smallest / len(cuts), largest / len(cuts)))
        level = level * jnp.repeat(draws, dims[axis_at] // shards_of).reshape([-1 if axis == axis_at else 1 for axis in range(len(dims))])
    return level


def gaussian(rng, shape, scale, most, cuts=(), kind=jnp.bfloat16):
    values = jax.random.normal(rng, shape, jnp.float32) * scale
    if len(cuts) > 0:
        values = shard_levels(rng, shape, cuts, -0.22, 0.18) * values
    return jnp.clip(values, min=-most, max=most).astype(kind)


def setup_inputs(seed: int = 0) -> dict:
    key_of = jax.random.split(jax.random.key(seed), 10)
    return {
        "features": gaussian(key_of[0], (CLIPS, FRAMES, H, W, C), 1.0, 6.0, ((1, 4), (2, 8))),
        "frame_counts": draw_frame_counts(jax.random.fold_in(key_of[9], 71), 0),
        "owner_order": jax.random.permutation(key_of[2], CLIPS).astype(jnp.int32),
        "first_gain": jnp.clip(1.0 + 0.18 * jax.random.normal(key_of[3], (C,), jnp.float32), 0.1, 1.9),
        "first_kernel": gaussian(key_of[4], (3, 3, 3, C, C), (27 * C) ** -0.5, 0.0625),
        "first_bias": gaussian(key_of[5], (C,), 0.5, 3.0, (), jnp.float32),
        "second_gain": jnp.clip(1.0 + 0.18 * jax.random.normal(key_of[6], (C,), jnp.float32), 0.1, 1.9),
        "second_kernel": gaussian(key_of[7], (3, 3, 3, C, C), (27 * C) ** -0.5, 0.0625),
        "second_bias": gaussian(key_of[8], (C,), 0.5, 3.0, (), jnp.float32),
    }


EPSILON = 1e-06

def normalize(source, norm_gain):
    values = source.astype(jnp.float32)
    factor = lax.rsqrt(lax.optimization_barrier(jnp.mean(values * values, axis=-1, keepdims=True)) + EPSILON)
    return jax.nn.silu(values * factor * norm_gain).astype(jnp.bfloat16)

def convolve(active, kernel, addend):
    frames, height, breadth, channels = active.shape
    padded = jnp.pad(active, ((2, 0), (1, 1), (1, 1), (0, 0)))
    running = jnp.zeros((frames * height * breadth, channels), jnp.float32)
    for height_tap in range(3):
        for width_tap in range(3):
            stacked = jnp.concatenate([padded[time_tap:time_tap + frames, height_tap:height_tap + height, width_tap:width_tap + breadth] for time_tap in range(3)], axis=-1)
            stacked = stacked.reshape(-1, 3 * channels)
            running = running + jnp.dot(stacked, kernel[:, height_tap, width_tap].reshape(3 * channels, channels), preferred_element_type=jnp.float32)
    return running.reshape(frames, height, breadth, channels) + addend

def reference(features, frame_counts, owner_order, first_gain, first_kernel, first_bias, second_gain, second_kernel, second_bias):

    def one_clip(packed):
        source, frame_count = packed
        usable = (jnp.arange(FRAMES) < frame_count).astype(jnp.float32)
        hidden = convolve(normalize(source, first_gain), first_kernel, first_bias).astype(jnp.bfloat16)
        result = convolve(normalize(hidden, second_gain), second_kernel, second_bias) + source.astype(jnp.float32)
        return result.astype(jnp.bfloat16) * usable.astype(jnp.bfloat16)[:, None, None, None]
    encoded = lax.map(one_clip, (features, frame_counts))
    return jnp.take(encoded, owner_order, axis=0)
```

```python
import jax
import jax.numpy as jnp
from jax import lax
from jax.sharding import PartitionSpec as P

EPSILON = 1e-06


def padded_2(shard, sides, width):
    for axis, dim in sides:
        peers, length = (lax.axis_size(axis), shard.shape[dim])
        up = [(i, (i + 1) % peers) for i in range(peers - 1)]
        down = [(j, i) for i, j in up]
        last = lax.slice_in_dim(shard, length - width, length, axis=dim)
        first = lax.slice_in_dim(shard, 0, width, axis=dim)
        before = lax.ppermute(last, axis, up)
        after = lax.ppermute(first, axis, down)
        shard = jnp.concatenate([before, shard, after], axis=dim)
    return shard


def normalize(block, norm_gain):
    values = block.astype(jnp.float32)
    factor = lax.rsqrt(jnp.mean(values * values, axis=-1, keepdims=True) + EPSILON)
    return jax.nn.silu(values * factor * norm_gain)


def extend(block):
    earlier = jnp.zeros_like(block[:, :2])
    joined = jnp.concatenate([earlier, block], axis=1)
    return padded_2(joined, (("rows", 2),), 1)


def convolve(extended, kernel, addend):
    clip_count = extended.shape[0]
    frames = extended.shape[1] - 2
    height = extended.shape[2] - 2
    breadth = extended.shape[3]
    channels = extended.shape[4]
    padded = jnp.pad(extended, ((0, 0), (0, 0), (0, 0), (1, 1), (0, 0)))
    running = jnp.zeros((clip_count * frames * height * breadth, channels), jnp.float32)
    for height_tap in range(3):
        for width_tap in range(3):
            stacked = jnp.concatenate(
                [
                    padded[
                        :,
                        time_tap : time_tap + frames,
                        height_tap : height_tap + height,
                        width_tap : width_tap + breadth,
                    ]
                    for time_tap in range(3)
                ],
                axis=-1,
            )
            stacked = stacked.reshape(-1, 3 * channels)
            running = running + jnp.dot(
                stacked,
                kernel[:, height_tap, width_tap].reshape(3 * channels, channels),
                preferred_element_type=jnp.float32,
            )
    return running.reshape(clip_count, frames, height, breadth, channels) + addend


def layer(block, norm_gain, kernel, addend):
    extended = extend(normalize(block, norm_gain).astype(jnp.bfloat16))
    return convolve(extended, kernel, addend)


def residual_block(
    local, usable, first_gain, first_kernel, first_bias, second_gain, second_kernel, second_bias
):
    hidden = layer(local, first_gain, first_kernel, first_bias).astype(jnp.bfloat16)
    result = layer(hidden, second_gain, second_kernel, second_bias) + local.astype(jnp.float32)
    return result.astype(jnp.bfloat16) * usable.astype(jnp.bfloat16)[:, :, None, None, None]


def per_device(
    features,
    frame_counts,
    owner_order,
    first_gain,
    first_kernel,
    first_bias,
    second_gain,
    second_kernel,
    second_bias,
):
    slab_index = lax.axis_index("tm")
    ordered = jnp.concatenate(
        [
            lax.dynamic_slice_in_dim(features, owner_order[slot], 1, axis=0)
            for slot in range(features.shape[0])
        ],
        axis=0,
    )
    local = lax.all_to_all(ordered, "tm", split_axis=0, concat_axis=1, tiled=True)
    slot_total = local.shape[0]
    slot_owners = lax.dynamic_slice_in_dim(owner_order, slab_index * slot_total, slot_total)
    slots = jnp.arange(frame_counts.shape[0], dtype=jnp.int32)
    owned = slot_owners[:, None] == slots[None, :]
    slot_counts = jnp.sum(jnp.where(owned, frame_counts[None, :], 0), axis=1)
    positions = jnp.arange(local.shape[1], dtype=jnp.int32)
    usable = (positions[None, :] < slot_counts[:, None]).astype(jnp.float32)
    result = residual_block(
        local, usable, first_gain, first_kernel, first_bias, second_gain, second_kernel, second_bias
    )
    return lax.all_to_all(result, "rows", split_axis=3, concat_axis=2, tiled=True)


def solution(mesh):
    placed = (P(None, "tm", "rows", None, None), P(), P(), P(), P(), P(), P(), P(), P())
    return jax.shard_map(
        per_device,
        mesh=mesh,
        in_specs=placed,
        out_specs=P("tm", None, None, "rows", None),
        check_vma=False,
    )
```

```python
import jax
import jax.numpy as jnp
import numpy as np
from jax import lax
from jax.experimental import pallas as pl
from jax.experimental.pallas import tpu as pltpu
from jax.sharding import PartitionSpec as P

EPSILON = 1e-06
HALO = 2
VMEM = 56 * 2**20


def one_hot(source, columns):
    table = np.asarray(source)[:, None] == np.arange(columns)[None, :]
    return jnp.asarray(table.astype(np.float32), jnp.bfloat16)


def permuted(table, rows):
    return jnp.dot(table, rows, preferred_element_type=jnp.float32).astype(jnp.bfloat16)


def permute_kernel(table_ref, rows_ref, out_ref):
    result = permuted(table_ref[...], rows_ref[...].reshape(-1, rows_ref.shape[-1]))
    out_ref[...] = result.reshape(out_ref.shape)


def pack(features, owner_order, bands):
    clips, frames, height, width, channels = features.shape
    rows, band = frames * height * width, width // bands
    places = np.arange(rows).reshape(frames * height, bands, band).transpose(1, 0, 2)
    return pl.pallas_call(
        lambda order_ref, *refs: permute_kernel(*refs),
        grid_spec=pltpu.PrefetchScalarGridSpec(
            num_scalar_prefetch=1,
            grid=(clips,),
            in_specs=[
                pl.BlockSpec((rows, rows), lambda k, order: (0, 0)),
                pl.BlockSpec((rows, channels), lambda k, order: (order[k], 0)),
            ],
            out_specs=pl.BlockSpec((rows, channels), lambda k, order: (k, 0)),
        ),
        out_shape=jax.ShapeDtypeStruct((clips * rows, channels), features.dtype),
    )(owner_order, one_hot(places.reshape(-1), rows), features.reshape(-1, channels))


def unpack(received, slabs, bands, frames, height, band):
    channels = received.shape[-1]
    rows = bands * frames * height * band
    places = np.arange(rows).reshape(bands, frames, height, band).transpose(1, 3, 0, 2)
    return pl.pallas_call(
        permute_kernel,
        grid=(slabs,),
        in_specs=[
            pl.BlockSpec((rows, rows), lambda s: (0, 0)),
            pl.BlockSpec((rows, channels), lambda s: (s, 0)),
        ],
        out_specs=pl.BlockSpec((frames, band, bands * height, channels), lambda s: (s, 0, 0, 0)),
        out_shape=jax.ShapeDtypeStruct(
            (slabs * frames, band, bands * height, channels), received.dtype
        ),
    )(one_hot(places.reshape(-1), rows), received)


def normalize(values, gain):
    factor = lax.rsqrt(jnp.mean(values * values, axis=-1, keepdims=True) + EPSILON)
    scaled = values * factor * gain
    return scaled / (1.0 + jnp.exp(-scaled))


def spread(active, taps_ref, height):
    rows, channels = active.shape
    place = lax.rem(lax.broadcasted_iota(jnp.int32, (rows, 1), 0), height)
    above = jnp.where(place == 0, 0.0, pltpu.roll(active, 1, 0))
    below = jnp.where(place == height - 1, 0.0, pltpu.roll(active, rows - 1, 0))
    kept = rows - 2 * height
    for row_tap, shifted in enumerate((above, active, below)):
        narrow = shifted.astype(jnp.bfloat16)
        for column_tap in range(3):
            at = (row_tap * 3 + column_tap) * channels
            taps_ref[:, at : at + channels] = narrow[column_tap * height : column_tap * height + kept]


def convolved(taps_ref, weights_ref, carry_ref, channels, reach):
    sums = jnp.dot(
        taps_ref[...], weights_ref[:, : reach * channels], preferred_element_type=jnp.float32
    )
    result = sums[:, :channels] + carry_ref[0]
    if reach > 1:
        carry_ref[0] = sums[:, channels : 2 * channels] + carry_ref[1]
    if reach > 2:
        carry_ref[1] = sums[:, 2 * channels :]
    return result


def block_kernel(
    info_ref,
    main_ref,
    left_ref,
    right_ref,
    first_kernel,
    second_kernel,
    first_gain,
    first_bias,
    second_gain,
    second_bias,
    table_ref,
    out_ref,
    first_weights,
    second_weights,
    first_taps,
    second_taps,
    first_carry,
    second_carry,
    arrived,
):
    frames, band, height, channels = main_ref.shape
    copies = [
        pltpu.make_async_copy(
            kernel.at[2 - ahead],
            weights.at[:, pl.ds(ahead * channels, channels)],
            arrived.at[which, ahead],
        )
        for which, (kernel, weights) in enumerate(
            ((first_kernel, first_weights), (second_kernel, second_weights))
        )
        for ahead in range(3)
    ]
    for copy in copies:
        copy.start()
    first_carry[...] = jnp.zeros_like(first_carry)
    second_carry[...] = jnp.zeros_like(second_carry)
    for copy in copies:
        copy.wait()

    inner = (band + 2) * height
    place = lax.broadcasted_iota(jnp.int32, (inner, 1), 0)
    outside = ((place < height) & (info_ref[1] == 1)) | (
        (place >= inner - height) & (info_ref[2] == 1)
    )

    def step(frame, reach):
        center = main_ref[frame].reshape(band * height, channels)
        source = jnp.concatenate(
            [
                left_ref[frame].reshape(HALO * height, channels),
                center,
                right_ref[frame].reshape(HALO * height, channels),
            ],
            axis=0,
        )
        spread(normalize(source.astype(jnp.float32), first_gain[...]), first_taps, height)
        hidden = convolved(first_taps, first_weights, first_carry, channels, reach)
        hidden = (hidden + first_bias[...]).astype(jnp.bfloat16).astype(jnp.float32)
        active = jnp.where(outside, 0.0, normalize(hidden, second_gain[...]))
        spread(active, second_taps, height)
        result = convolved(second_taps, second_weights, second_carry, channels, reach)
        result = result + second_bias[...] + center.astype(jnp.float32)
        result = jnp.where(frame < info_ref[0], result, 0.0).astype(jnp.bfloat16)
        placed = permuted(table_ref[...], result).reshape(height, -1, channels)
        out_ref[frame] = placed[:, :band]

    @pl.loop(0, frames - 2)
    def _(frame):
        step(frame, 3)

    step(frames - 2, 2)
    step(frames - 1, 1)


def block(info, main, left, right, kernels, gains, biases):
    frames, band, height, channels = main.shape
    padded = -(-band // 16) * 16
    places = np.full((height, padded), -1)
    places[:, :band] = np.arange(band * height).reshape(band, height).T
    table = one_hot(places.reshape(-1), band * height)
    taps = 9 * channels
    kernels = [k.reshape(3, taps, channels) for k in kernels]
    vectors = [v.reshape(1, channels) for pair in zip(gains, biases) for v in pair]
    whole = pl.BlockSpec(memory_space=pltpu.VMEM)
    anywhere = pl.BlockSpec(memory_space=pl.ANY)
    inner, outer = (band + 2) * height, band * height
    flops = 2 * 3 * taps * channels * frames * (inner + outer)
    return pl.pallas_call(
        block_kernel,
        in_specs=[pl.BlockSpec(memory_space=pltpu.SMEM)]
        + [whole] * 3
        + [anywhere] * 2
        + [whole] * 5,
        out_specs=whole,
        out_shape=jax.ShapeDtypeStruct((frames, height, band, channels), main.dtype),
        scratch_shapes=[
            pltpu.VMEM((taps, 3 * channels), jnp.bfloat16),
            pltpu.VMEM((taps, 3 * channels), jnp.bfloat16),
            pltpu.VMEM((inner, taps), jnp.bfloat16),
            pltpu.VMEM((outer, taps), jnp.bfloat16),
            pltpu.VMEM((2, inner, channels), jnp.float32),
            pltpu.VMEM((2, outer, channels), jnp.float32),
            pltpu.SemaphoreType.DMA((2, 3)),
        ],
        compiler_params=pltpu.CompilerParams(vmem_limit_bytes=VMEM),
        cost_estimate=pl.CostEstimate(flops=flops, bytes_accessed=20 * 2**20, transcendentals=0),
    )(info, main, left, right, *kernels, *vectors, table)


def per_device(
    features,
    frame_counts,
    owner_order,
    first_gain,
    first_kernel,
    first_bias,
    second_gain,
    second_kernel,
    second_bias,
):
    slabs, bands = lax.axis_size("tm"), lax.axis_size("rows")
    at = lax.axis_index("rows")
    frames, height = features.shape[1:3]
    band = features.shape[3] // bands
    packed = pack(features, owner_order, bands)
    received = lax.all_to_all(packed, ("tm", "rows"), split_axis=0, concat_axis=0, tiled=True)
    main = unpack(received, slabs, bands, frames, height, band)
    up = [(i, i + 1) for i in range(bands - 1)]
    left = lax.ppermute(main[:, band - HALO :], "rows", up)
    right = lax.ppermute(main[:, :HALO], "rows", [(j, i) for i, j in up])
    owner = lax.dynamic_index_in_dim(owner_order, lax.axis_index("tm"), 0, keepdims=False)
    clips = jnp.arange(frame_counts.shape[0], dtype=jnp.int32)
    count = jnp.sum(jnp.where(clips == owner, frame_counts, 0))
    info = jnp.stack([count, at == 0, at == bands - 1]).astype(jnp.int32)
    result = block(
        info,
        main,
        left,
        right,
        (first_kernel, second_kernel),
        (first_gain, second_gain),
        (first_bias, second_bias),
    )
    return result[None]


def solution(mesh):
    placed = (P(None, "tm", "rows", None, None), P(), P(), P(), P(), P(), P(), P(), P())
    return jax.shard_map(
        per_device,
        mesh=mesh,
        in_specs=placed,
        out_specs=P("tm", None, None, "rows", None),
        check_vma=False,
    )
```

```python
import jax
import jax.numpy as jnp
import numpy as np
from jax import lax
from jax.experimental import pallas as pl
from jax.experimental.pallas import tpu as pltpu
from jax.sharding import PartitionSpec as P

EPSILON = 1e-06
HALO = 2
VMEM = 58 * 2**20
SCALARS = pl.BlockSpec(memory_space=pltpu.SMEM)
WHOLE = pl.BlockSpec(memory_space=pltpu.VMEM)
ANYWHERE = pl.BlockSpec(memory_space=pl.ANY)


def one_hot(source, columns):
    return jnp.asarray(
        (np.asarray(source)[..., None] == np.arange(columns)).astype(np.float32), jnp.bfloat16
    )


def permuted(table, rows):
    return jnp.dot(table, rows, preferred_element_type=jnp.float32).astype(jnp.bfloat16)


def pack(features, owner_order, wanted):
    clips, frames, height, width, channels = features.shape
    bands = len(wanted)
    band, rows = width // bands, frames * height * width
    columns = np.asarray(wanted) + np.arange(bands)[:, None] * band
    places = np.arange(frames * height) * width + columns[:, :, None]
    places = np.where(((columns >= 0) & (columns < width))[:, :, None], places, -1).reshape(-1)

    def kernel(order_ref, table_ref, features_ref, out_ref):
        for slot in range(clips):
            source = features_ref[order_ref[slot]]
            out_ref[slot] = permuted(table_ref[...], source)

    packed = pl.pallas_call(
        kernel,
        in_specs=[SCALARS, WHOLE, WHOLE],
        out_specs=WHOLE,
        out_shape=jax.ShapeDtypeStruct((clips, len(places), channels), features.dtype),
        compiler_params=pltpu.CompilerParams(vmem_limit_bytes=VMEM // 4),
    )(owner_order, one_hot(places, rows), features.reshape(clips, rows, channels))
    return packed.reshape(-1, channels)


def unpack_table(parts, first, columns, bands, frames, height):
    tables = []
    for kind, start in enumerate(first):
        places = np.full((frames, columns, bands, height), -1)
        base = 0
        for held in parts:
            count = len(held[kind])
            rows = np.arange(bands * count * frames * height) + base
            rows = rows.reshape(bands, count, frames, height).transpose(2, 1, 0, 3)
            for at, column in enumerate(held[kind]):
                places[:, column - start] = rows[:, at]
            base += bands * count * frames * height
        tables.append(places.reshape(-1))
    return one_hot(np.stack(tables), base)


def normalize(values, gain):
    factor = lax.rsqrt(jnp.mean(values * values, axis=-1, keepdims=True) + EPSILON)
    scaled = values * factor * gain
    return scaled / (1.0 + jnp.exp(-scaled))


def spread(active, taps_ref, frame, height):
    rows, channels = active.shape
    place = lax.rem(lax.broadcasted_iota(jnp.int32, (rows, 1), 0), height)
    above = jnp.where(place == 0, 0.0, pltpu.roll(active, 1, 0))
    below = jnp.where(place == height - 1, 0.0, pltpu.roll(active, rows - 1, 0))
    kept = rows - 2 * height
    for row_tap, shifted in enumerate((above, active, below)):
        narrow = shifted.astype(jnp.bfloat16)
        for column_tap in range(3):
            at = (row_tap * 3 + column_tap) * channels
            taps_ref[frame, :kept, at : at + channels] = narrow[
                column_tap * height : column_tap * height + kept
            ]


def group(frames, rows):
    return max(g for g in range(1, frames + 1) if frames % g == 0 and (g == 1 or g * rows <= 640))


def multiply(taps_ref, weights_ref, copies, near_ref, far_ref, rows, channels):
    frames, _, taps = taps_ref.shape
    near_ref[0, :rows] = jnp.zeros((rows, 2 * channels), jnp.float32)
    far_ref[:2, :rows] = jnp.zeros((2, rows, channels), jnp.float32)

    def dots(count, sums_ref, skip, start, width):
        size = group(count, rows)

        @pl.loop(0, count // size)
        def _(step):
            operand = taps_ref[pl.ds(step * size, size), :rows].reshape(size * rows, taps)
            sums = jnp.dot(
                operand, weights_ref[:, start : start + width], preferred_element_type=jnp.float32
            )
            sums_ref[pl.ds(step * size + skip, size), :rows] = sums.reshape(size, rows, width)

    copies[0].wait()
    copies[1].wait()
    dots(frames, near_ref, 1, 0, 2 * channels)
    copies[2].wait()
    dots(frames - 2, far_ref, 2, 2 * channels, channels)


def added(near_ref, far_ref, frame, rows, channels):
    return (
        near_ref[frame + 1, :rows, :channels]
        + near_ref[frame, :rows, channels:]
        + far_ref[frame, :rows]
    )


def stage(
    owner_order,
    frame_counts,
    sources,
    table,
    saved,
    earlier,
    kernels,
    vectors,
    *,
    band,
    height,
    columns,
    new_at,
    saved_at,
    keep_at,
    center_at,
    out_at,
    edges,
    earlier_at=None,
):
    slabs, _, channels = sources[0].shape
    kinds, unpacked, _ = table.shape
    frames = slabs * (unpacked // (columns * height))
    taps = 9 * channels
    fresh = columns - 2
    window = fresh + (HALO if saved is not None else 0)
    made = window - 2
    inner, outer = fresh * height, made * height
    keeps, joins = keep_at is not None, earlier is not None

    def kernel(*refs):
        refs = list(refs)
        order_ref, counts_ref = refs.pop(0), refs.pop(0)
        source_refs = [refs.pop(0) for _ in sources]
        table_ref = refs.pop(0)
        saved_ref = refs.pop(0) if saved is not None else None
        earlier_ref = refs.pop(0) if joins else None
        kernel_refs = [refs.pop(0), refs.pop(0)]
        first_gain, first_bias, second_gain, second_bias = (refs.pop(0) for _ in range(4))
        out_ref = refs.pop(0)
        kept_ref = refs.pop(0) if keeps else None
        weights_refs = [refs.pop(0), refs.pop(0)]
        raw_ref, taps_ref, near_ref, far_ref, active_ref, arrived = refs[:6]
        result_ref, written = refs[6:] if joins else (out_ref, None)

        copies = [
            [
                pltpu.make_async_copy(
                    source.at[2 - ahead],
                    weights.at[:, pl.ds(ahead * channels, channels)],
                    arrived.at[which, ahead],
                )
                for ahead in range(3)
            ]
            for which, (source, weights) in enumerate(zip(kernel_refs, weights_refs))
        ]
        for copy in copies[0] + copies[1]:
            copy.start()

        at = lax.axis_index("rows")
        kind = lax.rem(at, kinds)

        def pick(places):
            return jnp.where(kind == 0, places[0], places[-1])

        moved = None
        if joins:
            moved = pltpu.make_async_copy(
                earlier_ref,
                out_ref.at[:, pl.ds(pick(earlier_at), earlier.shape[1])],
                written.at[frames],
            )
            moved.start()
        count = counts_ref[order_ref[lax.axis_index("tm")]]
        first_edge = edges & (at == 0)
        last_edge = edges & (at == lax.axis_size("rows") - 1)

        @pl.loop(0, slabs)
        def _(slab):
            rows = jnp.concatenate([source[slab] for source in source_refs], axis=0)
            placed = permuted(table_ref[kind], rows).reshape(-1, columns, height, channels)
            raw_ref[pl.ds(slab * placed.shape[0], placed.shape[0])] = placed

        @pl.loop(0, frames)
        def _(frame):
            values = raw_ref[frame].reshape(columns * height, channels).astype(jnp.float32)
            spread(normalize(values, first_gain[...]), taps_ref, frame, height)

        multiply(taps_ref, weights_refs[0], copies[0], near_ref, far_ref, inner, channels)
        place = lax.broadcasted_iota(jnp.int32, (inner, 1), 0)
        outside = ((place < height) & first_edge) | ((place >= inner - height) & last_edge)

        @pl.loop(0, frames)
        def _(frame):
            hidden = added(near_ref, far_ref, frame, inner, channels) + first_bias[...]
            hidden = hidden.astype(jnp.bfloat16).astype(jnp.float32)
            active = jnp.where(outside, 0.0, normalize(hidden, second_gain[...]))
            if saved is not None or keeps:
                active = active.reshape(fresh, height, channels)
                active_ref[pl.ds(pick(new_at), fresh)] = active
                if saved is not None:
                    active_ref[pl.ds(pick(saved_at), HALO)] = saved_ref[frame].astype(jnp.float32)
                if keeps:
                    kept = active_ref[pl.ds(pick(keep_at), HALO)]
                    kept_ref[frame] = kept.astype(jnp.bfloat16)
                active = active_ref[...].reshape(window * height, channels)
            spread(active, taps_ref, frame, height)

        multiply(taps_ref, weights_refs[1], copies[1], near_ref, far_ref, outer, channels)

        def write(frame):
            return pltpu.make_async_copy(
                result_ref.at[frame],
                out_ref.at[frame, pl.ds(pick(out_at), made)],
                written.at[frame],
            )

        @pl.loop(0, frames)
        def _(frame):
            center = raw_ref[frame, pl.ds(pick(center_at), made)].reshape(outer, channels)
            result = added(near_ref, far_ref, frame, outer, channels) + second_bias[...]
            result = result + center.astype(jnp.float32)
            result = jnp.where(frame < count, result, 0.0).astype(jnp.bfloat16)
            result_ref[frame] = result.reshape(made, height, channels)
            if joins:
                write(frame).start()

        if joins:
            moved.wait()

            @pl.loop(0, frames)
            def _(frame):
                write(frame).wait()

    out_shape = [
        jax.ShapeDtypeStruct((frames, band if joins else made, height, channels), jnp.bfloat16)
    ]
    if keeps:
        out_shape.append(jax.ShapeDtypeStruct((frames, HALO, height, channels), jnp.bfloat16))
    operands = [owner_order, frame_counts, *sources, table]
    specs = [SCALARS] * 2 + [WHOLE] * (len(sources) + 1)
    if saved is not None:
        operands.append(saved)
        specs.append(WHOLE)
    if joins:
        operands.append(earlier)
        specs.append(ANYWHERE)
    most = max(inner, outer)
    scratch = [
        pltpu.VMEM((taps, 3 * channels), jnp.bfloat16),
        pltpu.VMEM((taps, 3 * channels), jnp.bfloat16),
        pltpu.VMEM((frames, columns, height, channels), jnp.bfloat16),
        pltpu.VMEM((frames, most, taps), jnp.bfloat16),
        pltpu.VMEM((frames + 1, most, 2 * channels), jnp.float32),
        pltpu.VMEM((frames, most, channels), jnp.float32),
        pltpu.VMEM((window, height, channels), jnp.float32),
        pltpu.SemaphoreType.DMA((2, 3)),
    ]
    if joins:
        scratch += [
            pltpu.VMEM((frames, made, height, channels), jnp.bfloat16),
            pltpu.SemaphoreType.DMA((frames + 1,)),
        ]
    flops = 2 * 3 * taps * channels * frames * (inner + outer)
    return pl.pallas_call(
        kernel,
        in_specs=specs + [ANYWHERE] * 2 + [WHOLE] * 4,
        out_specs=[ANYWHERE if joins else WHOLE] + [WHOLE] * keeps,
        out_shape=out_shape,
        scratch_shapes=scratch,
        compiler_params=pltpu.CompilerParams(vmem_limit_bytes=VMEM),
        cost_estimate=pl.CostEstimate(flops=flops, bytes_accessed=20 * 2**20, transcendentals=0),
    )(*operands, *kernels, *vectors)


def exchange(packed):
    return lax.all_to_all(packed, ("tm", "rows"), split_axis=0, concat_axis=0, tiled=True)


def per_device(
    features,
    frame_counts,
    owner_order,
    first_gain,
    first_kernel,
    first_bias,
    second_gain,
    second_kernel,
    second_bias,
):
    slabs, bands = lax.axis_size("tm"), lax.axis_size("rows")
    frames, height = features.shape[1:3]
    channels = features.shape[4]
    band = features.shape[3] // bands
    cells = frames * height
    kernels = [k.reshape(3, 9 * channels, channels) for k in (first_kernel, second_kernel)]
    vectors = [
        v.reshape(1, channels) for v in (first_gain, first_bias, second_gain, second_bias)
    ]

    def slabbed(rows):
        return rows.reshape(slabs, -1, channels)

    def columns_of(received, count, start, stop):
        rows = received.reshape(slabs * bands, count * cells, channels)
        return rows[:, start * cells : stop * cells].reshape(-1, channels)

    common = dict(band=band, height=bands * height)
    later = band // 3
    if later >= HALO and bands % 2 == 0:
        soon = band - later
        order = (list(range(band - 1, -1 - HALO, -1)), list(range(band + HALO)))
        early = [columns[:soon] for columns in order]
        late = [columns[soon:] for columns in order]
        shared = [list(range(band, band + HALO)), list(range(-1, -1 - HALO, -1))]
        middle = [columns[-HALO:] for columns in early]
        wide, rest = soon + HALO, later + 2 * HALO

        received = exchange(pack(features, owner_order, [early[i % 2] for i in range(bands)]))
        packed = pack(features, owner_order, [late[i % 2] for i in range(bands)])
        received, packed = lax.optimization_barrier((received, packed))
        received_late = exchange(packed)
        halo = lax.ppermute(
            columns_of(received, soon, 0, HALO), "rows", [(i, i ^ 1) for i in range(bands)]
        )
        half, kept = stage(
            owner_order,
            frame_counts,
            [slabbed(received), slabbed(halo)],
            unpack_table((early, shared), (later, -HALO), wide, bands, frames, height),
            None,
            None,
            kernels,
            vectors,
            columns=wide,
            new_at=(0, 0),
            saved_at=None,
            keep_at=(0, soon - HALO),
            center_at=(2, 2),
            out_at=(later + 2, 0),
            edges=False,
            **common,
        )
        (result,) = stage(
            owner_order,
            frame_counts,
            [slabbed(received_late), slabbed(columns_of(received, soon, soon - HALO, soon))],
            unpack_table((late, middle), (-HALO, soon - HALO), rest, bands, frames, height),
            kept,
            half,
            kernels,
            vectors,
            columns=rest,
            new_at=(0, HALO),
            saved_at=(later + 2, 0),
            keep_at=None,
            center_at=(HALO, 0),
            out_at=(0, soon - 2),
            earlier_at=(later + 2, 0),
            edges=True,
            **common,
        )
    else:
        own = list(range(band))
        received = exchange(pack(features, owner_order, [own] * bands))
        up = [(i, i + 1) for i in range(bands - 1)]
        left = lax.ppermute(columns_of(received, band, band - HALO, band), "rows", up)
        right = lax.ppermute(columns_of(received, band, 0, HALO), "rows", [(j, i) for i, j in up])
        held = ([own], [list(range(-HALO, 0))], [list(range(band, band + HALO))])
        (result,) = stage(
            owner_order,
            frame_counts,
            [slabbed(received), slabbed(left), slabbed(right)],
            unpack_table(held, (-HALO,), band + 2 * HALO, bands, frames, height),
            None,
            None,
            kernels,
            vectors,
            columns=band + 2 * HALO,
            new_at=(0,),
            saved_at=None,
            keep_at=None,
            center_at=(HALO,),
            out_at=(0,),
            edges=True,
            **common,
        )
    return result.transpose(0, 2, 1, 3)[None]


def solution(mesh):
    placed = (P(None, "tm", "rows", None, None), P(), P(), P(), P(), P(), P(), P(), P())
    return jax.shard_map(
        per_device,
        mesh=mesh,
        in_specs=placed,
        out_specs=P("tm", None, None, "rows", None),
        check_vma=False,
    )
```

```python
import jax
import jax.numpy as jnp
import numpy as np
from jax import lax
from jax.experimental import pallas as pl
from jax.experimental.pallas import tpu as pltpu
from jax.sharding import PartitionSpec as P

EPSILON = 1e-06
HALO = 2
VMEM = 58 * 2**20
SPARE = 19 * 2**20
WHOLE = pl.BlockSpec(memory_space=pltpu.VMEM)
ANYWHERE = pl.BlockSpec(memory_space=pl.ANY)


def one_hot(source, columns):
    return jnp.asarray(
        (np.asarray(source)[..., None] == np.arange(columns)).astype(np.float32), jnp.bfloat16
    )


def permuted(table, rows):
    return jnp.dot(table, rows, preferred_element_type=jnp.float32).astype(jnp.bfloat16)


def pack(features, owner_order, wanted):
    clips, frames, height, width, channels = features.shape
    bands = len(wanted)
    band, rows = width // bands, frames * height * width
    columns = np.asarray(wanted) + np.arange(bands)[:, None] * band
    places = np.arange(frames * height) * width + columns[:, :, None]
    places = np.where(((columns >= 0) & (columns < width))[:, :, None], places, -1).reshape(-1)

    def kernel(order_ref, table_ref, features_ref, out_ref, table, sources, arrived):
        fetched = pltpu.make_async_copy(table_ref, table, arrived.at[clips])
        copies = [
            pltpu.make_async_copy(
                features_ref.at[order_ref[slot]], sources.at[slot], arrived.at[slot]
            )
            for slot in range(clips)
        ]
        for copy in [fetched] + copies:
            copy.start()
        fetched.wait()
        for slot, copy in enumerate(copies):
            copy.wait()
            out_ref[slot] = permuted(table[...], sources[slot])

    packed = pl.pallas_call(
        kernel,
        grid_spec=pltpu.PrefetchScalarGridSpec(
            num_scalar_prefetch=1,
            grid=(1,),
            in_specs=[ANYWHERE] * 2,
            out_specs=WHOLE,
            scratch_shapes=[
                pltpu.VMEM((len(places), rows), jnp.bfloat16),
                pltpu.VMEM((clips, rows, channels), jnp.bfloat16),
                pltpu.SemaphoreType.DMA((clips + 1,)),
            ],
        ),
        out_shape=jax.ShapeDtypeStruct((clips, len(places), channels), features.dtype),
        compiler_params=pltpu.CompilerParams(vmem_limit_bytes=VMEM),
    )(owner_order, one_hot(places, rows), features.reshape(clips, rows, channels))
    return packed.reshape(-1, channels)


def unpack_table(parts, first, columns, bands, frames, height):
    tables = []
    for kind, start in enumerate(first):
        places = np.full((frames, columns, bands, height), -1)
        base = 0
        for held in parts:
            count = len(held[kind])
            rows = np.arange(bands * count * frames * height) + base
            rows = rows.reshape(bands, count, frames, height).transpose(2, 1, 0, 3)
            for at, column in enumerate(held[kind]):
                places[:, column - start] = rows[:, at]
            base += bands * count * frames * height
        tables.append(places.reshape(-1))
    return one_hot(np.stack(tables), -(-base // 128) * 128)


def normalize(values, gain):
    factor = lax.rsqrt(jnp.mean(values * values, axis=-1, keepdims=True) + EPSILON)
    scaled = values * factor * gain
    return scaled / (1.0 + jnp.exp(-scaled))


def spread(active, taps_ref, frame, height):
    rows, channels = active.shape
    place = lax.rem(lax.broadcasted_iota(jnp.int32, (rows, 1), 0), height)
    above = jnp.where(place == 0, 0.0, pltpu.roll(active, 1, 0))
    below = jnp.where(place == height - 1, 0.0, pltpu.roll(active, rows - 1, 0))
    kept = rows - 2 * height
    for row_tap, shifted in enumerate((above, active, below)):
        narrow = shifted.astype(jnp.bfloat16)
        for column_tap in range(3):
            at = (row_tap * 3 + column_tap) * channels
            taps_ref[frame, :kept, at : at + channels] = narrow[
                column_tap * height : column_tap * height + kept
            ]


def group(frames, rows):
    return max(g for g in range(1, frames + 1) if frames % g == 0 and (g == 1 or g * rows <= 640))


def multiply(taps_ref, weights_ref, copies, near_ref, far_ref, rows, channels):
    frames, _, taps = taps_ref.shape
    near_ref[0, :rows] = jnp.zeros((rows, 2 * channels), jnp.float32)
    far_ref[:2, :rows] = jnp.zeros((2, rows, channels), jnp.float32)

    def dots(count, sums_ref, skip, start, width):
        size = group(count, rows)

        @pl.loop(0, count // size)
        def _(step):
            operand = taps_ref[pl.ds(step * size, size), :rows].reshape(size * rows, taps)
            sums = jnp.dot(
                operand, weights_ref[:, start : start + width], preferred_element_type=jnp.float32
            )
            sums_ref[pl.ds(step * size + skip, size), :rows] = sums.reshape(size, rows, width)

    copies[0].wait()
    copies[1].wait()
    dots(frames, near_ref, 1, 0, 2 * channels)
    copies[2].wait()
    dots(frames - 2, far_ref, 2, 2 * channels, channels)


def added(near_ref, far_ref, frame, rows, channels):
    return (
        near_ref[frame + 1, :rows, :channels]
        + near_ref[frame, :rows, channels:]
        + far_ref[frame, :rows]
    )


def stage(
    scalars,
    sources,
    table,
    saved,
    earlier,
    kernels,
    vectors,
    *,
    band,
    height,
    columns,
    new_at,
    saved_at,
    keep_at,
    center_at,
    out_at,
    edges,
    earlier_at=None,
):
    slabs, _, channels = sources[0].shape
    unpacked = table.shape[0]
    frames = slabs * (unpacked // (columns * height))
    taps = 9 * channels
    fresh = columns - 2
    window = fresh + (HALO if saved is not None else 0)
    made = window - 2
    inner, outer = fresh * height, made * height
    keeps, joins = keep_at is not None, earlier is not None

    def kernel(*refs):
        refs = list(refs)
        scalars_ref = refs.pop(0)
        source_refs = [refs.pop(0) for _ in sources]
        table_ref = refs.pop(0)
        saved_ref = refs.pop(0) if saved is not None else None
        earlier_ref = refs.pop(0) if joins else None
        kernel_refs = [refs.pop(0), refs.pop(0)]
        vectors_ref = refs.pop(0)
        first_gain, first_bias, second_gain, second_bias = (
            vectors_ref[i : i + 1] for i in range(4)
        )
        out_ref = refs.pop(0)
        kept_ref = refs.pop(0) if keeps else None
        weights_refs = [refs.pop(0), refs.pop(0)]
        raw_ref, taps_ref, near_ref, far_ref, active_ref, arrived = refs[:6]
        result_ref, held_ref, written = refs[6:] if joins else (out_ref, None, None)

        copies = [
            [
                pltpu.make_async_copy(
                    source.at[2 - ahead],
                    weights.at[:, pl.ds(ahead * channels, channels)],
                    arrived.at[which, ahead],
                )
                for ahead in range(3)
            ]
            for which, (source, weights) in enumerate(zip(kernel_refs, weights_refs))
        ]
        for copy in copies[0] + copies[1]:
            copy.start()

        at = lax.axis_index("rows")
        kind = lax.rem(at, 2)

        def pick(places):
            return jnp.where(kind == 0, places[0], places[-1])

        if joins:
            held = pltpu.make_async_copy(earlier_ref, held_ref, written.at[frames + 1])
            held.start()
            moved = pltpu.make_async_copy(
                held_ref,
                out_ref.at[:, pl.ds(pick(earlier_at), earlier.shape[1])],
                written.at[frames],
            )
        clips = scalars.shape[0] // 2
        count = scalars_ref[clips + scalars_ref[lax.axis_index("tm")]]
        first_edge = edges & (at == 0)
        last_edge = edges & (at == lax.axis_size("rows") - 1)

        @pl.loop(0, slabs)
        def _(slab):
            rows = [source[slab] for source in source_refs]
            spare = table_ref.shape[1] - sum(part.shape[0] for part in rows)
            if spare:
                rows.append(jnp.zeros((spare, channels), jnp.bfloat16))
            rows = jnp.concatenate(rows, axis=0)
            placed = permuted(table_ref[...], rows).reshape(-1, columns, height, channels)
            raw_ref[pl.ds(slab * placed.shape[0], placed.shape[0])] = placed

        @pl.loop(0, frames)
        def _(frame):
            values = raw_ref[frame].reshape(columns * height, channels).astype(jnp.float32)
            spread(normalize(values, first_gain), taps_ref, frame, height)

        multiply(taps_ref, weights_refs[0], copies[0], near_ref, far_ref, inner, channels)
        place = lax.broadcasted_iota(jnp.int32, (inner, 1), 0)
        outside = ((place < height) & first_edge) | ((place >= inner - height) & last_edge)

        @pl.loop(0, frames)
        def _(frame):
            hidden = added(near_ref, far_ref, frame, inner, channels) + first_bias
            hidden = hidden.astype(jnp.bfloat16).astype(jnp.float32)
            active = jnp.where(outside, 0.0, normalize(hidden, second_gain))
            if saved is not None or keeps:
                active = active.reshape(fresh, height, channels)
                active_ref[pl.ds(pick(new_at), fresh)] = active
                if saved is not None:
                    active_ref[pl.ds(pick(saved_at), HALO)] = saved_ref[frame].astype(jnp.float32)
                if keeps:
                    kept = active_ref[pl.ds(pick(keep_at), HALO)]
                    kept_ref[frame] = kept.astype(jnp.bfloat16)
                active = active_ref[...].reshape(window * height, channels)
            spread(active, taps_ref, frame, height)

        if joins:
            held.wait()
            moved.start()
        multiply(taps_ref, weights_refs[1], copies[1], near_ref, far_ref, outer, channels)

        def write(frame):
            return pltpu.make_async_copy(
                result_ref.at[frame],
                out_ref.at[frame, pl.ds(pick(out_at), made)],
                written.at[frame],
            )

        @pl.loop(0, frames)
        def _(frame):
            center = raw_ref[frame, pl.ds(pick(center_at), made)].reshape(outer, channels)
            result = added(near_ref, far_ref, frame, outer, channels) + second_bias
            result = result + center.astype(jnp.float32)
            result = jnp.where(frame < count, result, 0.0).astype(jnp.bfloat16)
            result_ref[frame] = result.reshape(made, height, channels)
            if joins:
                write(frame).start()

        if joins:
            moved.wait()

            @pl.loop(0, frames)
            def _(frame):
                write(frame).wait()

    out_shape = [
        jax.ShapeDtypeStruct((frames, band if joins else made, height, channels), jnp.bfloat16)
    ]
    if keeps:
        out_shape.append(jax.ShapeDtypeStruct((frames, HALO, height, channels), jnp.bfloat16))
    operands = [scalars, *sources, table]
    specs = [WHOLE] * (len(sources) + 1)
    if saved is not None:
        operands.append(saved)
        specs.append(WHOLE)
    if joins:
        operands.append(earlier)
        specs.append(ANYWHERE)
    most = max(inner, outer)
    scratch = [
        pltpu.VMEM((taps, 3 * channels), jnp.bfloat16),
        pltpu.VMEM((taps, 3 * channels), jnp.bfloat16),
        pltpu.VMEM((frames, columns, height, channels), jnp.bfloat16),
        pltpu.VMEM((frames, most, taps), jnp.bfloat16),
        pltpu.VMEM((frames + 1, most, 2 * channels), jnp.float32),
        pltpu.VMEM((frames, most, channels), jnp.float32),
        pltpu.VMEM((window, height, channels), jnp.float32),
        pltpu.SemaphoreType.DMA((2, 3)),
    ]
    if joins:
        scratch += [
            pltpu.VMEM((frames, made, height, channels), jnp.bfloat16),
            pltpu.VMEM(earlier.shape, jnp.bfloat16),
            pltpu.SemaphoreType.DMA((frames + 2,)),
        ]
    held = sum(
        int(np.prod(ref.shape)) * jnp.dtype(ref.dtype).itemsize
        for ref in scratch
        if len(ref.shape) > 2 or ref.shape[0] == taps
    )
    flops = 2 * 3 * taps * channels * frames * (inner + outer)
    return pl.pallas_call(
        kernel,
        grid_spec=pltpu.PrefetchScalarGridSpec(
            num_scalar_prefetch=1,
            grid=(1,),
            in_specs=specs + [ANYWHERE] * 2 + [WHOLE],
            out_specs=[ANYWHERE if joins else WHOLE] + [WHOLE] * keeps,
            scratch_shapes=scratch,
        ),
        out_shape=out_shape,
        compiler_params=pltpu.CompilerParams(vmem_limit_bytes=min(VMEM, held + SPARE)),
        cost_estimate=pl.CostEstimate(flops=flops, bytes_accessed=20 * 2**20, transcendentals=0),
    )(*operands, *kernels, vectors)


def exchange(packed):
    return lax.all_to_all(packed, ("tm", "rows"), split_axis=0, concat_axis=0, tiled=True)


def per_device(
    features,
    frame_counts,
    owner_order,
    first_gain,
    first_kernel,
    first_bias,
    second_gain,
    second_kernel,
    second_bias,
):
    slabs, bands = lax.axis_size("tm"), lax.axis_size("rows")
    frames, height = features.shape[1:3]
    channels = features.shape[4]
    band = features.shape[3] // bands
    cells = frames * height
    kernels = [k.reshape(3, 9 * channels, channels) for k in (first_kernel, second_kernel)]
    vectors = jnp.stack([first_gain, first_bias, second_gain, second_bias])
    scalars = jnp.concatenate([owner_order, frame_counts])

    def slabbed(rows):
        return rows.reshape(slabs, -1, channels)

    def columns_of(received, count, start, stop):
        rows = received.reshape(slabs * bands, count * cells, channels)
        return rows[:, start * cells : stop * cells].reshape(-1, channels)

    common = dict(band=band, height=bands * height)
    later = band // 3
    if later >= HALO and bands % 2 == 0:
        soon = band - later
        order = (list(range(band - 1, -1 - HALO, -1)), list(range(band + HALO)))
        early = [columns[:soon] for columns in order]
        late = [columns[soon:] for columns in order]
        shared = [list(range(band, band + HALO)), list(range(-1, -1 - HALO, -1))]
        middle = [columns[-HALO:] for columns in early]
        wide, rest = soon + HALO, later + 2 * HALO

        received = exchange(pack(features, owner_order, [early[i % 2] for i in range(bands)]))
        packed = pack(features, owner_order, [late[i % 2] for i in range(bands)])
        early_table, late_table = (
            lax.dynamic_index_in_dim(tables, lax.rem(lax.axis_index("rows"), 2), 0, keepdims=False)
            for tables in (
                unpack_table((early, shared), (later, -HALO), wide, bands, frames, height),
                unpack_table((late, middle), (-HALO, soon - HALO), rest, bands, frames, height),
            )
        )
        received, packed, scalars, vectors, early_table, late_table = lax.optimization_barrier(
            (received, packed, scalars, vectors, early_table, late_table)
        )
        received_late = exchange(packed)
        halo = lax.ppermute(
            columns_of(received, soon, 0, HALO), "rows", [(i, i ^ 1) for i in range(bands)]
        )
        half, kept = stage(
            scalars,
            [slabbed(received), slabbed(halo)],
            early_table,
            None,
            None,
            kernels,
            vectors,
            columns=wide,
            new_at=(0, 0),
            saved_at=None,
            keep_at=(0, soon - HALO),
            center_at=(2, 2),
            out_at=(later + 2, 0),
            edges=False,
            **common,
        )
        (result,) = stage(
            scalars,
            [slabbed(received_late), slabbed(columns_of(received, soon, soon - HALO, soon))],
            late_table,
            kept,
            half,
            kernels,
            vectors,
            columns=rest,
            new_at=(0, HALO),
            saved_at=(later + 2, 0),
            keep_at=None,
            center_at=(HALO, 0),
            out_at=(0, soon - 2),
            earlier_at=(later + 2, 0),
            edges=True,
            **common,
        )
    else:
        own = list(range(band))
        received = exchange(pack(features, owner_order, [own] * bands))
        up = [(i, i + 1) for i in range(bands - 1)]
        left = lax.ppermute(columns_of(received, band, band - HALO, band), "rows", up)
        right = lax.ppermute(columns_of(received, band, 0, HALO), "rows", [(j, i) for i, j in up])
        held = ([own], [list(range(-HALO, 0))], [list(range(band, band + HALO))])
        (result,) = stage(
            scalars,
            [slabbed(received), slabbed(left), slabbed(right)],
            unpack_table(held, (-HALO,), band + 2 * HALO, bands, frames, height)[0],
            None,
            None,
            kernels,
            vectors,
            columns=band + 2 * HALO,
            new_at=(0,),
            saved_at=None,
            keep_at=None,
            center_at=(HALO,),
            out_at=(0,),
            edges=True,
            **common,
        )
    return result.transpose(0, 2, 1, 3)[None]


def solution(mesh):
    placed = (P(None, "tm", "rows", None, None), P(), P(), P(), P(), P(), P(), P(), P())
    return jax.shard_map(
        per_device,
        mesh=mesh,
        in_specs=placed,
        out_specs=P("tm", None, None, "rows", None),
        check_vma=False,
    )
```

```python
import jax
import jax.numpy as jnp
import numpy as np
from jax import lax
from jax.experimental import pallas as pl
from jax.experimental.pallas import tpu as pltpu
from jax.sharding import PartitionSpec as P

EPSILON = 1e-06
HALO = 2
VMEM = 58 * 2**20
SPARE = 19 * 2**20
WHOLE = pl.BlockSpec(memory_space=pltpu.VMEM)
ANYWHERE = pl.BlockSpec(memory_space=pl.ANY)


def one_hot(source, columns):
    return jnp.asarray(
        (np.asarray(source)[..., None] == np.arange(columns)).astype(np.float32), jnp.bfloat16
    )


def permuted(table, rows):
    return jnp.dot(table, rows, preferred_element_type=jnp.float32).astype(jnp.bfloat16)


def pack(features, owner_order, wanted):
    clips, frames, height, width, channels = features.shape
    bands = len(wanted)
    band, rows = width // bands, frames * height * width
    columns = np.asarray(wanted) + np.arange(bands)[:, None] * band
    places = np.arange(frames * height) * width + columns[:, :, None]
    places = np.where(((columns >= 0) & (columns < width))[:, :, None], places, -1).reshape(-1)

    def kernel(order_ref, table_ref, features_ref, out_ref, table, sources, arrived):
        fetched = pltpu.make_async_copy(table_ref, table, arrived.at[clips])
        copies = [
            pltpu.make_async_copy(
                features_ref.at[order_ref[slot]], sources.at[slot], arrived.at[slot]
            )
            for slot in range(clips)
        ]
        for copy in [fetched] + copies:
            copy.start()
        fetched.wait()
        for slot, copy in enumerate(copies):
            copy.wait()
            out_ref[slot] = permuted(table[...], sources[slot])

    packed = pl.pallas_call(
        kernel,
        grid_spec=pltpu.PrefetchScalarGridSpec(
            num_scalar_prefetch=1,
            grid=(1,),
            in_specs=[ANYWHERE] * 2,
            out_specs=WHOLE,
            scratch_shapes=[
                pltpu.VMEM((len(places), rows), jnp.bfloat16),
                pltpu.VMEM((clips, rows, channels), jnp.bfloat16),
                pltpu.SemaphoreType.DMA((clips + 1,)),
            ],
        ),
        out_shape=jax.ShapeDtypeStruct((clips, len(places), channels), features.dtype),
        compiler_params=pltpu.CompilerParams(vmem_limit_bytes=VMEM),
    )(owner_order, one_hot(places, rows), features.reshape(clips, rows, channels))
    return packed.reshape(-1, channels)


def unpack_table(parts, first, columns, bands, frames, height):
    tables = []
    for kind, start in enumerate(first):
        places = np.full((frames, columns, bands, height), -1)
        base = 0
        for held in parts:
            count = len(held[kind])
            rows = np.arange(bands * count * frames * height) + base
            rows = rows.reshape(bands, count, frames, height).transpose(2, 1, 0, 3)
            for at, column in enumerate(held[kind]):
                places[:, column - start] = rows[:, at]
            base += bands * count * frames * height
        tables.append(places.reshape(-1))
    return one_hot(np.stack(tables), -(-base // 128) * 128)


def normalize(values, gain):
    factor = lax.rsqrt(jnp.mean(values * values, axis=-1, keepdims=True) + EPSILON)
    scaled = values * factor * gain
    return scaled / (1.0 + jnp.exp(-scaled))


def spread(active, taps_ref, frame, height):
    rows, channels = active.shape
    place = lax.rem(lax.broadcasted_iota(jnp.int32, (rows, 1), 0), height)
    above = jnp.where(place == 0, 0.0, pltpu.roll(active, 1, 0))
    below = jnp.where(place == height - 1, 0.0, pltpu.roll(active, rows - 1, 0))
    kept = rows - 2 * height
    for row_tap, shifted in enumerate((above, active, below)):
        narrow = shifted.astype(jnp.bfloat16)
        for column_tap in range(3):
            at = (row_tap * 3 + column_tap) * channels
            taps_ref[frame, :kept, at : at + channels] = narrow[
                column_tap * height : column_tap * height + kept
            ]


def group(frames, rows, most):
    sizes = [g for g in range(1, most + 1) if frames % g == 0]
    return max(g for g in sizes if g == 1 or g * rows <= 640)


def multiply(taps_ref, weights_ref, copies, near_ref, far_ref, rows, channels, beside_near, beside_far):
    frames, _, taps = taps_ref.shape
    near_ref[0, :rows] = jnp.zeros((rows, 2 * channels), jnp.float32)
    far_ref[:2, :rows] = jnp.zeros((2, rows, channels), jnp.float32)

    def dots(count, sums_ref, skip, start, width, beside):
        size = group(count, rows, count // 2)
        for first in range(0, count, size):
            operand = taps_ref[first : first + size, :rows].reshape(size * rows, taps)
            sums = jnp.dot(
                operand, weights_ref[:, start : start + width], preferred_element_type=jnp.float32
            )
            sums_ref[first + skip : first + skip + size, :rows] = sums.reshape(size, rows, width)
            beside(first, size, first + size == count)

    copies[0].wait()
    copies[1].wait()
    dots(frames, near_ref, 1, 0, 2 * channels, beside_near)
    copies[2].wait()
    dots(frames - 2, far_ref, 2, 2 * channels, channels, beside_far)


def added(near_ref, far_ref, frame, rows, channels):
    return (
        near_ref[frame + 1, :rows, :channels]
        + near_ref[frame, :rows, channels:]
        + far_ref[frame, :rows]
    )


def stage(
    scalars,
    sources,
    table,
    saved,
    earlier,
    kernels,
    vectors,
    *,
    band,
    height,
    columns,
    new_at,
    saved_at,
    keep_at,
    center_at,
    out_at,
    edges,
    earlier_at=None,
):
    slabs, _, channels = sources[0].shape
    unpacked = table.shape[0]
    frames = slabs * (unpacked // (columns * height))
    taps = 9 * channels
    fresh = columns - 2
    window = fresh + (HALO if saved is not None else 0)
    made = window - 2
    inner, outer = fresh * height, made * height
    keeps, joins = keep_at is not None, earlier is not None

    def kernel(*refs):
        refs = list(refs)
        scalars_ref = refs.pop(0)
        source_refs = [refs.pop(0) for _ in sources]
        table_ref = refs.pop(0)
        saved_ref = refs.pop(0) if saved is not None else None
        earlier_ref = refs.pop(0) if joins else None
        kernel_refs = [refs.pop(0), refs.pop(0)]
        vectors_ref = refs.pop(0)
        first_gain, first_bias, second_gain, second_bias = (
            vectors_ref[i : i + 1] for i in range(4)
        )
        out_ref = refs.pop(0)
        kept_ref = refs.pop(0) if keeps else None
        weights_refs = [refs.pop(0), refs.pop(0)]
        raw_ref, taps_ref, near_ref, far_ref, active_ref, arrived = refs[:6]
        result_ref, held_ref, written = refs[6:] if joins else (out_ref, None, None)

        copies = [
            [
                pltpu.make_async_copy(
                    source.at[2 - ahead],
                    weights.at[:, pl.ds(ahead * channels, channels)],
                    arrived.at[which, ahead],
                )
                for ahead in range(3)
            ]
            for which, (source, weights) in enumerate(zip(kernel_refs, weights_refs))
        ]
        for copy in copies[0] + copies[1]:
            copy.start()

        at = lax.axis_index("rows")
        kind = lax.rem(at, 2)

        def pick(places):
            return jnp.where(kind == 0, places[0], places[-1])

        if joins:
            held = pltpu.make_async_copy(earlier_ref, held_ref, written.at[frames + 1])
            held.start()
            moved = pltpu.make_async_copy(
                held_ref,
                out_ref.at[:, pl.ds(pick(earlier_at), earlier.shape[1])],
                written.at[frames],
            )
        clips = scalars.shape[0] // 2
        count = scalars_ref[clips + scalars_ref[lax.axis_index("tm")]]
        first_edge = edges & (at == 0)
        last_edge = edges & (at == lax.axis_size("rows") - 1)

        @pl.loop(0, slabs)
        def _(slab):
            rows = [source[slab] for source in source_refs]
            spare = table_ref.shape[1] - sum(part.shape[0] for part in rows)
            if spare:
                rows.append(jnp.zeros((spare, channels), jnp.bfloat16))
            rows = jnp.concatenate(rows, axis=0)
            placed = permuted(table_ref[...], rows).reshape(-1, columns, height, channels)
            raw_ref[pl.ds(slab * placed.shape[0], placed.shape[0])] = placed

        def prepare(frame):
            values = raw_ref[frame].reshape(columns * height, channels).astype(jnp.float32)
            spread(normalize(values, first_gain), taps_ref, frame, height)

        def hide(frame):
            hidden = added(near_ref, far_ref, frame, inner, channels) + first_bias
            hidden = hidden.astype(jnp.bfloat16).astype(jnp.float32)
            active = normalize(hidden, second_gain)
            if edges:
                place = lax.broadcasted_iota(jnp.int32, (inner, 1), 0)
                outside = (place < height) & first_edge
                outside |= (place >= inner - height) & last_edge
                active = jnp.where(outside, 0.0, active)
            if saved is not None or keeps:
                active = active.reshape(fresh, height, channels)
                active_ref[pl.ds(pick(new_at), fresh)] = active
                if saved is not None:
                    active_ref[pl.ds(pick(saved_at), HALO)] = saved_ref[frame].astype(jnp.float32)
                if keeps:
                    kept = active_ref[pl.ds(pick(keep_at), HALO)]
                    kept_ref[frame] = kept.astype(jnp.bfloat16)
                active = active_ref[...].reshape(window * height, channels)
            spread(active, taps_ref, frame, height)

        def write(frame):
            return pltpu.make_async_copy(
                result_ref.at[frame],
                out_ref.at[frame, pl.ds(pick(out_at), made)],
                written.at[frame],
            )

        def finish(frame):
            center = raw_ref[frame, pl.ds(pick(center_at), made)].reshape(outer, channels)
            result = added(near_ref, far_ref, frame, outer, channels) + second_bias
            result = result + center.astype(jnp.float32)
            result = jnp.where(frame < count, result, 0.0).astype(jnp.bfloat16)
            result_ref[frame] = result.reshape(made, height, channels)
            if joins:
                write(frame).start()

        done = {prepare: 0, hide: 0, finish: 0}

        def through(work, stop, unrolled=True):
            start, done[work] = done[work], max(done[work], min(stop, frames))
            if unrolled:
                for frame in range(start, done[work]):
                    work(frame)
            elif start < done[work]:
                pl.loop(start, done[work])(work)

        first_size = group(frames, inner, frames // 2)
        second_size = group(frames, outer, frames // 2)
        through(prepare, first_size, False)
        multiply(
            taps_ref,
            weights_refs[0],
            copies[0],
            near_ref,
            far_ref,
            inner,
            channels,
            lambda first, size, last: through(prepare, first + 2 * size),
            lambda first, size, last: through(hide, first if last else 0),
        )
        through(hide, second_size + 1, False)
        if joins:
            held.wait()
            moved.start()
        multiply(
            taps_ref,
            weights_refs[1],
            copies[1],
            near_ref,
            far_ref,
            outer,
            channels,
            lambda first, size, last: through(hide, frames),
            lambda first, size, last: through(finish, first + 2 if last else 0),
        )
        through(finish, frames, False)
        if joins:
            moved.wait()

            @pl.loop(0, frames)
            def _(frame):
                write(frame).wait()

    out_shape = [
        jax.ShapeDtypeStruct((frames, band if joins else made, height, channels), jnp.bfloat16)
    ]
    if keeps:
        out_shape.append(jax.ShapeDtypeStruct((frames, HALO, height, channels), jnp.bfloat16))
    operands = [scalars, *sources, table]
    specs = [WHOLE] * (len(sources) + 1)
    if saved is not None:
        operands.append(saved)
        specs.append(WHOLE)
    if joins:
        operands.append(earlier)
        specs.append(ANYWHERE)
    most = max(inner, outer)
    scratch = [
        pltpu.VMEM((taps, 3 * channels), jnp.bfloat16),
        pltpu.VMEM((taps, 3 * channels), jnp.bfloat16),
        pltpu.VMEM((frames, columns, height, channels), jnp.bfloat16),
        pltpu.VMEM((frames, most, taps), jnp.bfloat16),
        pltpu.VMEM((frames + 1, most, 2 * channels), jnp.float32),
        pltpu.VMEM((frames, most, channels), jnp.float32),
        pltpu.VMEM((window, height, channels), jnp.float32),
        pltpu.SemaphoreType.DMA((2, 3)),
    ]
    if joins:
        scratch += [
            pltpu.VMEM((frames, made, height, channels), jnp.bfloat16),
            pltpu.VMEM(earlier.shape, jnp.bfloat16),
            pltpu.SemaphoreType.DMA((frames + 2,)),
        ]
    held = sum(
        int(np.prod(ref.shape)) * jnp.dtype(ref.dtype).itemsize
        for ref in scratch
        if len(ref.shape) > 2 or ref.shape[0] == taps
    )
    flops = 2 * 3 * taps * channels * frames * (inner + outer)
    return pl.pallas_call(
        kernel,
        grid_spec=pltpu.PrefetchScalarGridSpec(
            num_scalar_prefetch=1,
            grid=(1,),
            in_specs=specs + [ANYWHERE] * 2 + [WHOLE],
            out_specs=[ANYWHERE if joins else WHOLE] + [WHOLE] * keeps,
            scratch_shapes=scratch,
        ),
        out_shape=out_shape,
        compiler_params=pltpu.CompilerParams(vmem_limit_bytes=min(VMEM, held + SPARE)),
        cost_estimate=pl.CostEstimate(flops=flops, bytes_accessed=20 * 2**20, transcendentals=0),
    )(*operands, *kernels, vectors)


def exchange(packed):
    return lax.all_to_all(packed, ("tm", "rows"), split_axis=0, concat_axis=0, tiled=True)


def per_device(
    features,
    frame_counts,
    owner_order,
    first_gain,
    first_kernel,
    first_bias,
    second_gain,
    second_kernel,
    second_bias,
):
    slabs, bands = lax.axis_size("tm"), lax.axis_size("rows")
    frames, height = features.shape[1:3]
    channels = features.shape[4]
    band = features.shape[3] // bands
    cells = frames * height
    kernels = [k.reshape(3, 9 * channels, channels) for k in (first_kernel, second_kernel)]
    vectors = jnp.stack([first_gain, first_bias, second_gain, second_bias])
    scalars = jnp.concatenate([owner_order, frame_counts])

    def slabbed(rows):
        return rows.reshape(slabs, -1, channels)

    def columns_of(received, count, start, stop):
        rows = received.reshape(slabs * bands, count * cells, channels)
        return rows[:, start * cells : stop * cells].reshape(-1, channels)

    common = dict(band=band, height=bands * height)
    later = band // 3
    if later >= HALO and bands % 2 == 0:
        soon = band - later
        order = (list(range(band - 1, -1 - HALO, -1)), list(range(band + HALO)))
        early = [columns[:soon] for columns in order]
        late = [columns[soon:] for columns in order]
        shared = [list(range(band, band + HALO)), list(range(-1, -1 - HALO, -1))]
        middle = [columns[-HALO:] for columns in early]
        wide, rest = soon + HALO, later + 2 * HALO

        received = exchange(pack(features, owner_order, [early[i % 2] for i in range(bands)]))
        packed = pack(features, owner_order, [late[i % 2] for i in range(bands)])
        early_table, late_table = (
            lax.dynamic_index_in_dim(tables, lax.rem(lax.axis_index("rows"), 2), 0, keepdims=False)
            for tables in (
                unpack_table((early, shared), (later, -HALO), wide, bands, frames, height),
                unpack_table((late, middle), (-HALO, soon - HALO), rest, bands, frames, height),
            )
        )
        received, packed, scalars, vectors, early_table, late_table = lax.optimization_barrier(
            (received, packed, scalars, vectors, early_table, late_table)
        )
        received_late = exchange(packed)
        halo = lax.ppermute(
            columns_of(received, soon, 0, HALO), "rows", [(i, i ^ 1) for i in range(bands)]
        )
        half, kept = stage(
            scalars,
            [slabbed(received), slabbed(halo)],
            early_table,
            None,
            None,
            kernels,
            vectors,
            columns=wide,
            new_at=(0, 0),
            saved_at=None,
            keep_at=(0, soon - HALO),
            center_at=(2, 2),
            out_at=(later + 2, 0),
            edges=False,
            **common,
        )
        (result,) = stage(
            scalars,
            [slabbed(received_late), slabbed(columns_of(received, soon, soon - HALO, soon))],
            late_table,
            kept,
            half,
            kernels,
            vectors,
            columns=rest,
            new_at=(0, HALO),
            saved_at=(later + 2, 0),
            keep_at=None,
            center_at=(HALO, 0),
            out_at=(0, soon - 2),
            earlier_at=(later + 2, 0),
            edges=True,
            **common,
        )
    else:
        own = list(range(band))
        received = exchange(pack(features, owner_order, [own] * bands))
        up = [(i, i + 1) for i in range(bands - 1)]
        left = lax.ppermute(columns_of(received, band, band - HALO, band), "rows", up)
        right = lax.ppermute(columns_of(received, band, 0, HALO), "rows", [(j, i) for i, j in up])
        held = ([own], [list(range(-HALO, 0))], [list(range(band, band + HALO))])
        (result,) = stage(
            scalars,
            [slabbed(received), slabbed(left), slabbed(right)],
            unpack_table(held, (-HALO,), band + 2 * HALO, bands, frames, height)[0],
            None,
            None,
            kernels,
            vectors,
            columns=band + 2 * HALO,
            new_at=(0,),
            saved_at=None,
            keep_at=None,
            center_at=(HALO,),
            out_at=(0,),
            edges=True,
            **common,
        )
    return result.transpose(0, 2, 1, 3)[None]


def solution(mesh):
    placed = (P(None, "tm", "rows", None, None), P(), P(), P(), P(), P(), P(), P(), P())
    return jax.shard_map(
        per_device,
        mesh=mesh,
        in_specs=placed,
        out_specs=P("tm", None, None, "rows", None),
        check_vma=False,
    )
```

```python
import jax
import jax.numpy as jnp
import numpy as np
from jax import lax
from jax.experimental import pallas as pl
from jax.experimental.pallas import tpu as pltpu
from jax.sharding import PartitionSpec as P

EPSILON = 1e-06
HALO = 2
VMEM = 58 * 2**20
SPARE = 19 * 2**20
WHOLE = pl.BlockSpec(memory_space=pltpu.VMEM)
ANYWHERE = pl.BlockSpec(memory_space=pl.ANY)


def one_hot(source, columns):
    return jnp.asarray(
        (np.asarray(source)[..., None] == np.arange(columns)).astype(np.float32), jnp.bfloat16
    )


def permuted(table, rows):
    return jnp.dot(table, rows, preferred_element_type=jnp.float32).astype(jnp.bfloat16)


def pack(features, owner_order, wanted):
    clips, frames, height, width, channels = features.shape
    bands = len(wanted)
    band, rows = width // bands, frames * height * width
    columns = np.asarray(wanted) + np.arange(bands)[:, None] * band
    places = np.arange(frames * height) * width + columns[:, :, None]
    places = np.where(((columns >= 0) & (columns < width))[:, :, None], places, -1).reshape(-1)

    def kernel(order_ref, table_ref, features_ref, out_ref, table, sources, packed, arrived, left):
        fetched = pltpu.make_async_copy(table_ref, table, arrived.at[clips])
        copies = [
            pltpu.make_async_copy(
                features_ref.at[order_ref[slot]], sources.at[slot], arrived.at[slot]
            )
            for slot in range(clips)
        ]
        for copy in [fetched] + copies:
            copy.start()
        fetched.wait()
        for slot, copy in enumerate(copies):
            copy.wait()
            packed[slot] = permuted(table[...], sources[slot])
            pltpu.make_async_copy(packed.at[slot], out_ref.at[slot], left.at[slot]).start()
        for slot in range(clips):
            pltpu.make_async_copy(packed.at[slot], out_ref.at[slot], left.at[slot]).wait()

    packed = pl.pallas_call(
        kernel,
        grid_spec=pltpu.PrefetchScalarGridSpec(
            num_scalar_prefetch=1,
            grid=(1,),
            in_specs=[ANYWHERE] * 2,
            out_specs=ANYWHERE,
            scratch_shapes=[
                pltpu.VMEM((len(places), rows), jnp.bfloat16),
                pltpu.VMEM((clips, rows, channels), jnp.bfloat16),
                pltpu.VMEM((clips, len(places), channels), jnp.bfloat16),
                pltpu.SemaphoreType.DMA((clips + 1,)),
                pltpu.SemaphoreType.DMA((clips,)),
            ],
        ),
        out_shape=jax.ShapeDtypeStruct((clips, len(places), channels), features.dtype),
        compiler_params=pltpu.CompilerParams(vmem_limit_bytes=VMEM),
    )(owner_order, one_hot(places, rows), features.reshape(clips, rows, channels))
    return packed.reshape(-1, channels)


def unpack_table(parts, first, columns, bands, frames, height):
    tables = []
    for kind, start in enumerate(first):
        places = np.full((frames, columns, bands, height), -1)
        base = 0
        for held in parts:
            count = len(held[kind])
            rows = np.arange(bands * count * frames * height) + base
            rows = rows.reshape(bands, count, frames, height).transpose(2, 1, 0, 3)
            for at, column in enumerate(held[kind]):
                places[:, column - start] = rows[:, at]
            base += bands * count * frames * height
        tables.append(places.reshape(-1))
    return one_hot(np.stack(tables), -(-base // 128) * 128)


def normalize(values, gain):
    factor = lax.rsqrt(jnp.mean(values * values, axis=-1, keepdims=True) + EPSILON)
    scaled = values * factor * gain
    return scaled / (1.0 + jnp.exp(-scaled))


def spread(active, taps_ref, frame, height):
    rows, channels = active.shape
    place = lax.rem(lax.broadcasted_iota(jnp.int32, (rows, 1), 0), height)
    above = jnp.where(place == 0, 0.0, pltpu.roll(active, 1, 0))
    below = jnp.where(place == height - 1, 0.0, pltpu.roll(active, rows - 1, 0))
    kept = rows - 2 * height
    first = frame * kept if isinstance(frame, int) else pl.multiple_of(frame * kept, kept)
    for row_tap, shifted in enumerate((above, active, below)):
        narrow = shifted.astype(jnp.bfloat16)
        for column_tap in range(3):
            at = (row_tap * 3 + column_tap) * channels
            taps_ref[pl.ds(first, kept), at : at + channels] = narrow[
                column_tap * height : column_tap * height + kept
            ]


def group(frames, rows, most):
    sizes = [g for g in range(1, most + 1) if frames % g == 0]
    return max(g for g in sizes if g == 1 or g * rows <= 640)


def multiply(taps_ref, weights_ref, copies, near_ref, far_ref, rows, channels, beside_near, beside_far):
    frames = far_ref.shape[0]
    near_ref[0, :rows] = jnp.zeros((rows, 2 * channels), jnp.float32)
    far_ref[:2, :rows] = jnp.zeros((2, rows, channels), jnp.float32)

    def dots(count, sums_ref, skip, start, width, beside):
        size = group(count, rows, count // 2)
        for first in range(0, count, size):
            operand = taps_ref[first * rows : (first + size) * rows]
            sums = jnp.dot(
                operand, weights_ref[:, start : start + width], preferred_element_type=jnp.float32
            )
            sums_ref[first + skip : first + skip + size, :rows] = sums.reshape(size, rows, width)
            beside(first, size, first + size == count)

    copies[0].wait()
    copies[1].wait()
    dots(frames, near_ref, 1, 0, 2 * channels, beside_near)
    copies[2].wait()
    dots(frames - 2, far_ref, 2, 2 * channels, channels, beside_far)


def added(near_ref, far_ref, frame, rows, channels):
    return (
        near_ref[frame + 1, :rows, :channels]
        + near_ref[frame, :rows, channels:]
        + far_ref[frame, :rows]
    )


def stage(
    scalars,
    sources,
    table,
    saved,
    earlier,
    kernels,
    vectors,
    *,
    band,
    height,
    columns,
    new_at,
    saved_at,
    keep_at,
    center_at,
    out_at,
    edges,
    earlier_at=None,
):
    slabs, _, channels = sources[0].shape
    unpacked = table.shape[0]
    frames = slabs * (unpacked // (columns * height))
    taps = 9 * channels
    fresh = columns - 2
    window = fresh + (HALO if saved is not None else 0)
    made = window - 2
    inner, outer = fresh * height, made * height
    keeps, joins = keep_at is not None, earlier is not None

    def kernel(*refs):
        refs = list(refs)
        scalars_ref = refs.pop(0)
        source_refs = [refs.pop(0) for _ in sources]
        table_ref = refs.pop(0)
        saved_ref = refs.pop(0) if saved is not None else None
        earlier_ref = refs.pop(0) if joins else None
        kernel_refs = [refs.pop(0), refs.pop(0)]
        vectors_ref = refs.pop(0)
        first_gain, first_bias, second_gain, second_bias = (
            vectors_ref[i : i + 1] for i in range(4)
        )
        out_ref = refs.pop(0)
        kept_ref = refs.pop(0) if keeps else None
        weights_refs = [refs.pop(0), refs.pop(0)]
        raw_ref, taps_ref, near_ref, far_ref, active_ref, arrived = refs[:6]
        result_ref, held_ref, written = refs[6:] if joins else (out_ref, None, None)

        copies = [
            [
                pltpu.make_async_copy(
                    source.at[2 - ahead],
                    weights.at[:, pl.ds(ahead * channels, channels)],
                    arrived.at[which, ahead],
                )
                for ahead in range(3)
            ]
            for which, (source, weights) in enumerate(zip(kernel_refs, weights_refs))
        ]
        for copy in copies[0] + copies[1]:
            copy.start()

        at = lax.axis_index("rows")
        kind = lax.rem(at, 2)

        def pick(places):
            return jnp.where(kind == 0, places[0], places[-1])

        if joins:
            held = pltpu.make_async_copy(earlier_ref, held_ref, written.at[frames + 1])
            held.start()
            moved = pltpu.make_async_copy(
                held_ref,
                out_ref.at[:, pl.ds(pick(earlier_at), earlier.shape[1])],
                written.at[frames],
            )
        clips = scalars.shape[0] // 2
        count = scalars_ref[clips + scalars_ref[lax.axis_index("tm")]]
        first_edge = edges & (at == 0)
        last_edge = edges & (at == lax.axis_size("rows") - 1)

        @pl.loop(0, slabs)
        def _(slab):
            rows = [source[slab] for source in source_refs]
            spare = table_ref.shape[1] - sum(part.shape[0] for part in rows)
            if spare:
                rows.append(jnp.zeros((spare, channels), jnp.bfloat16))
            rows = jnp.concatenate(rows, axis=0)
            placed = permuted(table_ref[...], rows).reshape(-1, columns, height, channels)
            raw_ref[pl.ds(slab * placed.shape[0], placed.shape[0])] = placed

        def prepare(frame):
            values = raw_ref[frame].reshape(columns * height, channels).astype(jnp.float32)
            spread(normalize(values, first_gain), taps_ref, frame, height)

        def hide(frame):
            hidden = added(near_ref, far_ref, frame, inner, channels) + first_bias
            hidden = hidden.astype(jnp.bfloat16).astype(jnp.float32)
            active = normalize(hidden, second_gain)
            if edges:
                place = lax.broadcasted_iota(jnp.int32, (inner, 1), 0)
                outside = (place < height) & first_edge
                outside |= (place >= inner - height) & last_edge
                active = jnp.where(outside, 0.0, active)
            if saved is not None or keeps:
                active = active.reshape(fresh, height, channels)
                active_ref[pl.ds(pick(new_at), fresh)] = active
                if saved is not None:
                    active_ref[pl.ds(pick(saved_at), HALO)] = saved_ref[frame].astype(jnp.float32)
                if keeps:
                    kept = active_ref[pl.ds(pick(keep_at), HALO)]
                    kept_ref[frame] = kept.astype(jnp.bfloat16)
                active = active_ref[...].reshape(window * height, channels)
            spread(active, taps_ref, frame, height)

        def write(frame):
            return pltpu.make_async_copy(
                result_ref.at[frame],
                out_ref.at[frame, pl.ds(pick(out_at), made)],
                written.at[frame],
            )

        def finish(frame):
            center = raw_ref[frame, pl.ds(pick(center_at), made)].reshape(outer, channels)
            result = added(near_ref, far_ref, frame, outer, channels) + second_bias
            result = result + center.astype(jnp.float32)
            result = jnp.where(frame < count, result, 0.0).astype(jnp.bfloat16)
            result_ref[frame] = result.reshape(made, height, channels)
            if joins:
                write(frame).start()

        done = {prepare: 0, hide: 0, finish: 0}

        def through(work, stop, unrolled=True):
            start, done[work] = done[work], max(done[work], min(stop, frames))
            if unrolled:
                for frame in range(start, done[work]):
                    work(frame)
            elif start < done[work]:
                pl.loop(start, done[work])(work)

        first_size = group(frames, inner, frames // 2)
        second_size = group(frames, outer, frames // 2)
        through(prepare, first_size, False)
        multiply(
            taps_ref,
            weights_refs[0],
            copies[0],
            near_ref,
            far_ref,
            inner,
            channels,
            lambda first, size, last: through(prepare, first + 2 * size),
            lambda first, size, last: through(hide, first if last else 0),
        )
        through(hide, second_size + 1, False)
        if joins:
            held.wait()
            moved.start()
        multiply(
            taps_ref,
            weights_refs[1],
            copies[1],
            near_ref,
            far_ref,
            outer,
            channels,
            lambda first, size, last: through(hide, frames),
            lambda first, size, last: through(finish, first + 2 if last else 0),
        )
        through(finish, frames, False)
        if joins:
            moved.wait()

            @pl.loop(0, frames)
            def _(frame):
                write(frame).wait()

    out_shape = [
        jax.ShapeDtypeStruct((frames, band if joins else made, height, channels), jnp.bfloat16)
    ]
    if keeps:
        out_shape.append(jax.ShapeDtypeStruct((frames, HALO, height, channels), jnp.bfloat16))
    operands = [scalars, *sources, table]
    specs = [WHOLE] * (len(sources) + 1)
    if saved is not None:
        operands.append(saved)
        specs.append(WHOLE)
    if joins:
        operands.append(earlier)
        specs.append(ANYWHERE)
    most = max(inner, outer)
    scratch = [
        pltpu.VMEM((taps, 3 * channels), jnp.bfloat16),
        pltpu.VMEM((taps, 3 * channels), jnp.bfloat16),
        pltpu.VMEM((frames, columns, height, channels), jnp.bfloat16),
        pltpu.VMEM((frames * most, taps), jnp.bfloat16),
        pltpu.VMEM((frames + 1, most, 2 * channels), jnp.float32),
        pltpu.VMEM((frames, most, channels), jnp.float32),
        pltpu.VMEM((window, height, channels), jnp.float32),
        pltpu.SemaphoreType.DMA((2, 3)),
    ]
    if joins:
        scratch += [
            pltpu.VMEM((frames, made, height, channels), jnp.bfloat16),
            pltpu.VMEM(earlier.shape, jnp.bfloat16),
            pltpu.SemaphoreType.DMA((frames + 2,)),
        ]
    held = sum(
        int(np.prod(ref.shape)) * jnp.dtype(ref.dtype).itemsize
        for ref in scratch
        if len(ref.shape) > 1 and ref.shape != (2, 3)
    )
    flops = 2 * 3 * taps * channels * frames * (inner + outer)
    return pl.pallas_call(
        kernel,
        grid_spec=pltpu.PrefetchScalarGridSpec(
            num_scalar_prefetch=1,
            grid=(1,),
            in_specs=specs + [ANYWHERE] * 2 + [WHOLE],
            out_specs=[ANYWHERE if joins else WHOLE] + [WHOLE] * keeps,
            scratch_shapes=scratch,
        ),
        out_shape=out_shape,
        compiler_params=pltpu.CompilerParams(vmem_limit_bytes=min(VMEM, held + SPARE)),
        cost_estimate=pl.CostEstimate(flops=flops, bytes_accessed=20 * 2**20, transcendentals=0),
    )(*operands, *kernels, vectors)


def exchange(packed):
    return lax.all_to_all(packed, ("tm", "rows"), split_axis=0, concat_axis=0, tiled=True)


def per_device(
    features,
    frame_counts,
    owner_order,
    first_gain,
    first_kernel,
    first_bias,
    second_gain,
    second_kernel,
    second_bias,
):
    slabs, bands = lax.axis_size("tm"), lax.axis_size("rows")
    frames, height = features.shape[1:3]
    channels = features.shape[4]
    band = features.shape[3] // bands
    cells = frames * height
    kernels = [k.reshape(3, 9 * channels, channels) for k in (first_kernel, second_kernel)]
    vectors = jnp.stack([first_gain, first_bias, second_gain, second_bias])
    scalars = jnp.concatenate([owner_order, frame_counts])

    def slabbed(rows):
        return rows.reshape(slabs, -1, channels)

    def columns_of(received, count, start, stop):
        rows = received.reshape(slabs * bands, count * cells, channels)
        return rows[:, start * cells : stop * cells].reshape(-1, channels)

    common = dict(band=band, height=bands * height)
    later = band // 3
    if later >= HALO and bands % 2 == 0:
        soon = band - later
        order = (list(range(band - 1, -1 - HALO, -1)), list(range(band + HALO)))
        early = [columns[:soon] for columns in order]
        late = [columns[soon:] for columns in order]
        shared = [list(range(band, band + HALO)), list(range(-1, -1 - HALO, -1))]
        middle = [columns[-HALO:] for columns in early]
        wide, rest = soon + HALO, later + 2 * HALO

        received = exchange(pack(features, owner_order, [early[i % 2] for i in range(bands)]))
        packed = pack(features, owner_order, [late[i % 2] for i in range(bands)])
        early_table, late_table = (
            lax.dynamic_index_in_dim(tables, lax.rem(lax.axis_index("rows"), 2), 0, keepdims=False)
            for tables in (
                unpack_table((early, shared), (later, -HALO), wide, bands, frames, height),
                unpack_table((late, middle), (-HALO, soon - HALO), rest, bands, frames, height),
            )
        )
        received, packed, scalars, vectors, early_table, late_table = lax.optimization_barrier(
            (received, packed, scalars, vectors, early_table, late_table)
        )
        received_late = exchange(packed)
        halo = lax.ppermute(
            columns_of(received, soon, 0, HALO), "rows", [(i, i ^ 1) for i in range(bands)]
        )
        half, kept = stage(
            scalars,
            [slabbed(received), slabbed(halo)],
            early_table,
            None,
            None,
            kernels,
            vectors,
            columns=wide,
            new_at=(0, 0),
            saved_at=None,
            keep_at=(0, soon - HALO),
            center_at=(2, 2),
            out_at=(later + 2, 0),
            edges=False,
            **common,
        )
        (result,) = stage(
            scalars,
            [slabbed(received_late), slabbed(columns_of(received, soon, soon - HALO, soon))],
            late_table,
            kept,
            half,
            kernels,
            vectors,
            columns=rest,
            new_at=(0, HALO),
            saved_at=(later + 2, 0),
            keep_at=None,
            center_at=(HALO, 0),
            out_at=(0, soon - 2),
            earlier_at=(later + 2, 0),
            edges=True,
            **common,
        )
    else:
        own = list(range(band))
        received = exchange(pack(features, owner_order, [own] * bands))
        up = [(i, i + 1) for i in range(bands - 1)]
        left = lax.ppermute(columns_of(received, band, band - HALO, band), "rows", up)
        right = lax.ppermute(columns_of(received, band, 0, HALO), "rows", [(j, i) for i, j in up])
        held = ([own], [list(range(-HALO, 0))], [list(range(band, band + HALO))])
        (result,) = stage(
            scalars,
            [slabbed(received), slabbed(left), slabbed(right)],
            unpack_table(held, (-HALO,), band + 2 * HALO, bands, frames, height)[0],
            None,
            None,
            kernels,
            vectors,
            columns=band + 2 * HALO,
            new_at=(0,),
            saved_at=None,
            keep_at=None,
            center_at=(HALO,),
            out_at=(0,),
            edges=True,
            **common,
        )
    return result.transpose(0, 2, 1, 3)[None]


def solution(mesh):
    placed = (P(None, "tm", "rows", None, None), P(), P(), P(), P(), P(), P(), P(), P())
    return jax.shard_map(
        per_device,
        mesh=mesh,
        in_specs=placed,
        out_specs=P("tm", None, None, "rows", None),
        check_vma=False,
    )
```
